32 devices in a mesh: groups: 2 (over x), sec: 16 (over z, y, core).
Axes of the slice: x: 2, y: 2, z: 4, core: 2. Of those that a mesh axis runs over, the one named last changes fastest.
Arguments:
- hidden_rows: bfloat16 [128, 7168], P(('groups', 'sec')), parts along dimension 0, may hold values from -6 to 6
- residual: bfloat16 [128, 7168], P(('groups', 'sec')), parts along dimension 0, may hold values from -2 to 2
- expert_ids: int32 [128, 3], P(('groups', 'sec')), parts along dimension 0, may hold values from 0 to 7, all different within a row; in each aligned block of 4 rows (0 to 3, 4 to 7, ...) at most 2 rows name the same one
- router_logits: float32 [128, 3], P(('groups', 'sec')), parts along dimension 0, may hold values from -6 to 6
- w_gate: bfloat16 [7168, 32768], P(None, 'sec'), may hold values from -0.0625 to 0.0625
- w_up: bfloat16 [7168, 32768], P(None, 'sec'), may hold values from -0.0625 to 0.0625
- w_down: bfloat16 [32768, 7168], P('sec'), may hold values from -0.09375 to 0.09375
- queries: bfloat16 [256, 16384], P(('groups', 'sec')), parts along dimension 0, may hold values from -200 to 200
- new_kv: bfloat16 [256, 512], P(('groups', 'sec')), parts along dimension 0, may hold values from -6 to 6
- kv_cache: bfloat16 [256, 64, 512], P(('groups', 'sec')), parts along dimension 0, may hold values from -6 to 6
- cache_slot: int32 [32, 8], P(('groups', 'sec')), parts along dimension 0, may hold values from 0 to 7, each once within a row
- cache_lengths: int32 [256], P(('groups', 'sec')), parts along dimension 0, may hold values from 1 to 64, as said below
Outputs:
- mixed: bfloat16 [128, 7168], P(('groups', 'sec')), parts along dimension 0
- attended: bfloat16 [256, 16384], P(('groups', 'sec')), parts along dimension 0
The draws below stay inside these ranges and needn't reach their ends.
There are 2 independent parts, one for each index of `groups`. The reference program is written for one: setup_inputs(seed, part) draws one part's arguments, and reference() takes and returns one part's arrays. A program takes and returns all parts, laid end to end along the dimension named above; an argument that names none is the same for every part. Nothing has to cross between parts.
Inputs may be any that keep to these rules, and one draw needn't show every extreme that they name: `expert_ids`: in the rows of one device no expert is named more than 2 times; each row names 3 different experts. `cache_lengths`: some request has all 64 positions cached. `cache_slot`: each device's row is an ordering of its 8 slots.
All inputs are finite; a program needn't handle non-finite values.
Results may differ from the reference program's by a relative error of at most 0.0057.
Values may be sent and summed in bfloat16 or wider, within the bound.
A program may use at most 192 MiB of HBM per device.

```python
import math
import jax
import jax.numpy as jnp
import numpy as np
from jax import lax

D = 7168
HEADS = 64
HEAD = 256
FF = 4096
EXPERTS = 8
TOP = 3
TOK_DEV = 4
REQ_DEV = 8
CTX = 64
CAP = 2
TOKENS = 64
REQUESTS = 128
BLOCKS = 16
N_SEC = 16


def draw_queries(key, part):
    key = jax.random.fold_in(key, 11)
    base = jnp.clip(jax.random.normal(jax.random.fold_in(key, 1), (REQUESTS, HEADS, HEAD), jnp.float32), -4.0, 4.0)
    return base.reshape(REQUESTS, HEADS * HEAD).astype(jnp.bfloat16)


def draw_cache_lengths(key, part):
    key = jax.random.fold_in(key, 21)
    values = jax.random.randint(jax.random.fold_in(key, 1), (REQUESTS,), 1, CTX + 1, jnp.int32)
    target = jax.random.randint(jax.random.fold_in(key, 2), (), 0, REQUESTS, jnp.int32)
    filled = jnp.where(jnp.arange(REQUESTS, dtype=jnp.int32) == target, CTX, values)
    return filled.astype(jnp.int32)


def level_of(rng, shape, cuts, smallest, high):
    def one(dim, blocks):
        heights = jax.random.uniform(jax.random.fold_in(jax.random.fold_in(rng, 6), dim), (blocks,), jnp.float32, smallest / len(cuts), high / len(cuts))
        return jnp.repeat(jnp.exp(heights), shape[dim] // blocks).reshape((-1,) + (1,) * (len(shape) - dim - 1))

    gain = one(*cuts[0])
    for cut in cuts[1:]:
        gain = gain * one(*cut)
    return gain


def shared_out(key, own, number, rows, number_of, top, limit, lean):
    ranking = jax.random.permutation(key, number_of)
    crowded, common = load_shares(number_of, rows * top, limit, lean, True), load_shares(number_of, rows * top, limit, lean, False)
    places = jnp.arange(number_of)

    def named(lengths, offset_by):
        used = int((lengths > 0).sum())
        fixed = max(1, used // 4)
        passed = fixed + (places - fixed + offset_by * (used - fixed)) % max(1, number_of - fixed)
        return jnp.zeros((number_of,), jnp.int32).at[ranking[jnp.where(places < fixed, places, passed)]].set(jnp.asarray(lengths, jnp.int32))

    lengths = jnp.where(number % 4 == 0, named(crowded, number // 4), named(common, number - number // 4 - 1))
    mixed = jax.random.permutation(jax.random.fold_in(own, 3), number_of)
    source_of, receiver = mixed[0:number_of // 2 * 2:2], mixed[1:number_of // 2 * 2:2]
    slack = jnp.minimum(lengths[source_of] - 1, limit - lengths[receiver]) // 2
    slack = jnp.where((source_of == ranking[0]) | (receiver == ranking[0]) | (lengths[receiver] == 0), 0, jnp.maximum(slack, 0))
    passed = jax.random.randint(jax.random.fold_in(own, 4), (number_of // 2,), 0, 1 << 20) % (slack + 1)
    lengths = lengths.at[source_of].add(-passed).at[receiver].add(passed)
    members = jnp.searchsorted(jnp.cumsum(lengths), jnp.arange(rows * top), side="right").astype(jnp.int32)
    grid = members.reshape(top, rows).T
    grid = grid[jax.random.permutation(jax.random.fold_in(own, 1), rows)]
    offset_by = jax.random.randint(jax.random.fold_in(own, 2), (rows, 1), 0, top)
    return jnp.take_along_axis(grid, (jnp.arange(top)[None, :] + offset_by) % top, axis=1)


def load_shares(number_of, total, reach, skew, full):
    weights = [(1 << 20) // math.isqrt(standing ** skew) + 1 for standing in range(1, number_of + 1)]
    largest = reach if full else min(reach, max(-(-total // number_of), total * weights[0] // sum(weights)))
    least = 1 if total - largest >= number_of - 1 else 0
    given, rest = [largest] + [least] * (number_of - 1), total - largest - least * (number_of - 1)
    while rest > 0:
        candidates = [i for i in range(1, number_of) if given[i] < largest] or [i for i in range(1, number_of) if given[i] < reach]
        whole, left = sum([weights[i] for i in candidates]), rest
        for i in candidates:
            addition = min(reach - given[i], max(1, left * weights[i] // whole), rest)
            given[i] = given[i] + addition
            rest = rest - addition
    return np.array(given)


def centred(key, dims, scale, most, cuts=(), kind=jnp.bfloat16):
    values = scale * jax.random.normal(key, dims, jnp.float32)
    if cuts:
        values = values * level_of(key, dims, cuts, -0.22, 0.18)
    return jnp.clip(values, -most, most).astype(kind)


def setup_inputs(seed: int = 0, part: int = 0) -> dict:
    keys = jax.random.split(jax.random.key(seed), 13)
    part_keys = jax.random.split(jax.random.fold_in(keys[12], part), 13)
    hidden_rows = centred(part_keys[0], (TOKENS, D), 1.0, 6.0, ((0, 16),))
    residual = centred(part_keys[1], (TOKENS, D), 0.3, 2.0, ((0, 16),))
    expert_ids_keys = jax.random.split(jax.random.fold_in(part_keys[2], 1), TOKENS // TOK_DEV)
    expert_ids_turns = jax.random.permutation(jax.random.fold_in(part_keys[2], 3), TOKENS // TOK_DEV)
    expert_ids = jax.vmap(lambda own, number: shared_out(jax.random.fold_in(part_keys[2], 2), own, number, TOK_DEV, EXPERTS, TOP, CAP, 1))(expert_ids_keys, expert_ids_turns).reshape((TOKENS, TOP))
    router_logits = centred(part_keys[3], (TOKENS, TOP), 1.5, 6.0, ((0, 16),), jnp.float32)
    w_gate = centred(keys[4], (D, EXPERTS * FF), D ** -0.5, 0.0625, ((1, 16),))
    w_up = centred(keys[5], (D, EXPERTS * FF), D ** -0.5, 0.0625, ((1, 16),))
    w_down = centred(keys[6], (EXPERTS * FF, D), FF ** -0.5, 0.09375, ((0, 16),))
    queries = draw_queries(jax.random.fold_in(jax.random.fold_in(keys[12], part), 71), part)
    new_kv = centred(part_keys[8], (REQUESTS, 2 * HEAD), 1.0, 6.0, ((0, 16),))
    kv_cache = centred(part_keys[9], (REQUESTS, CTX, 2 * HEAD), 1.0, 6.0, ((0, 16),))
    cache_slot = jax.vmap(lambda own: jax.random.permutation(own, REQ_DEV))(jax.random.split(part_keys[10], BLOCKS)).reshape((BLOCKS, REQ_DEV)).astype(jnp.int32)
    cache_lengths = draw_cache_lengths(jax.random.fold_in(jax.random.fold_in(keys[12], part), 71), part)
    return {"hidden_rows": hidden_rows, "residual": residual, "expert_ids": expert_ids, "router_logits": router_logits, "w_gate": w_gate, "w_up": w_up, "w_down": w_down, "queries": queries, "new_kv": new_kv, "kv_cache": kv_cache, "cache_slot": cache_slot, "cache_lengths": cache_lengths}


NEG_FILL = -1e+30

def slot_codes(expert_ids):
    flattened = expert_ids.reshape(-1)
    onehot = (flattened[:, None] == jnp.arange(EXPERTS, dtype=jnp.int32)[None, :]).astype(jnp.int32)
    earlier = jnp.cumsum(onehot, axis=0) - onehot
    position = lax.optimization_barrier(jnp.sum(earlier * onehot, axis=1))
    return (flattened * CAP + position).reshape(expert_ids.shape).astype(jnp.int32)

def expert_block(buffer, expert_index, w_gate, w_up, w_down):
    shards = N_SEC // EXPERTS
    hidden_each = FF // shards

    def one_shard(carry, shard_index):
        start = (expert_index * FF + shard_index * hidden_each).astype(jnp.int32)
        gate_cols = lax.dynamic_slice_in_dim(w_gate, start, hidden_each, 1)
        up_cols = lax.dynamic_slice_in_dim(w_up, start, hidden_each, 1)
        down_rows = lax.dynamic_slice_in_dim(w_down, start, hidden_each, 0)
        gate_proj = jnp.dot(buffer, gate_cols, preferred_element_type=jnp.float32)
        up_proj = jnp.dot(buffer, up_cols, preferred_element_type=jnp.float32)
        activated = (jax.nn.silu(gate_proj) * up_proj).astype(jnp.bfloat16)
        partial_value = jnp.dot(activated, down_rows, preferred_element_type=jnp.float32).astype(jnp.bfloat16)
        return (carry + partial_value.astype(jnp.float32), None)
    initial = jnp.zeros((buffer.shape[0], D), jnp.float32)
    summed, unused = lax.scan(one_shard, initial, jnp.arange(shards, dtype=jnp.int32))
    return summed

def reference(hidden_rows, residual, expert_ids, router_logits, w_gate, w_up, w_down, queries, new_kv, kv_cache, cache_slot, cache_lengths):
    blocks = N_SEC
    coded = jax.vmap(slot_codes)(expert_ids.reshape(blocks, TOK_DEV, TOP))
    expert_of = (coded // CAP).astype(jnp.int32)
    position = (coded % CAP).astype(jnp.int32)
    block_index = jnp.arange(blocks, dtype=jnp.int32)[:, None, None]
    row_index = (block_index * CAP + position).astype(jnp.int32)
    spread = jnp.broadcast_to(hidden_rows.reshape(blocks, TOK_DEV, 1, D), (blocks, TOK_DEV, TOP, D))
    buffers = jnp.zeros((EXPERTS, blocks * CAP, D), jnp.bfloat16)
    buffers = buffers.at[expert_of.reshape(-1), row_index.reshape(-1)].set(spread.reshape(-1, D))

    def run_expert(pair):
        return expert_block(pair[0], pair[1], w_gate, w_up, w_down)
    outputs = lax.map(run_expert, (buffers, jnp.arange(EXPERTS, dtype=jnp.int32)))
    chosen = outputs[expert_of.reshape(-1), row_index.reshape(-1)].reshape(TOKENS, TOP, D)
    raised = jax.nn.sigmoid(router_logits)
    gate_weight = raised / lax.optimization_barrier(jnp.sum(raised, axis=1, keepdims=True))
    mixed = (residual.astype(jnp.float32) + lax.optimization_barrier(jnp.sum(gate_weight[:, :, None] * chosen, axis=1))).astype(jnp.bfloat16)
    global_rows = (jnp.arange(blocks, dtype=jnp.int32)[:, None] * REQ_DEV + cache_slot).reshape(-1).astype(jnp.int32)
    cache_rows = kv_cache[global_rows]
    query_heads = queries.reshape(REQUESTS, HEADS, HEAD).astype(jnp.float32)
    cache_keys = cache_rows[:, :, :HEAD].astype(jnp.float32)
    cache_values = cache_rows[:, :, HEAD:].astype(jnp.float32)
    new_key = new_kv[:, :HEAD].astype(jnp.float32)
    new_value = new_kv[:, HEAD:].astype(jnp.float32)
    inverse_root = 1.0 / math.sqrt(HEAD)
    scores = jnp.einsum('rhd,rcd->rhc', query_heads, cache_keys) * inverse_root
    own_score = jnp.einsum('rhd,rd->rh', query_heads, new_key) * inverse_root
    visible = jnp.arange(CTX, dtype=jnp.int32)[None, None, :] < cache_lengths[:, None, None]
    scores = jnp.where(visible, scores, NEG_FILL)
    row_max = jnp.maximum(lax.optimization_barrier(jnp.max(scores, axis=2)), own_score)
    lifted = jnp.where(visible, jnp.exp(scores - row_max[:, :, None]), 0.0)
    own_lift = jnp.exp(own_score - row_max)
    denominator = lax.optimization_barrier(jnp.sum(lifted, axis=2)) + own_lift
    weights_bf = (lifted / denominator[:, :, None]).astype(jnp.bfloat16)
    own_bf = (own_lift / denominator).astype(jnp.bfloat16)
    combined = jnp.einsum('rhc,rcd->rhd', weights_bf.astype(jnp.float32), cache_values)
    combined = combined + own_bf.astype(jnp.float32)[:, :, None] * new_value[:, None, :]
    attended = combined.astype(jnp.bfloat16).reshape(REQUESTS, HEADS * HEAD)
    return (mixed, attended)
```

```python
import functools
import math

import jax
import jax.numpy as jnp
from jax import lax
from jax.experimental import pallas as pl
from jax.experimental.pallas import tpu as pltpu
from jax.sharding import PartitionSpec as P

EXPERTS = 8
TOP = 3
CAP = 2

NEG_FILL = -1e30

LANES = 128
SUB = 8
BLOCK = SUB * LANES
VMEM_BYTES = 63 * 1024 * 1024
SLOTS = 28
HEADS_STEP = 16
MESH = pl.DeviceIdType.MESH


def iota(shape, dim):
    return lax.broadcasted_iota(jnp.int32, shape, dim)


def layer_kernel(
    chips,
    ids_ref,
    logits_ref,
    new_ref,
    slot_ref,
    length_ref,
    hidden_hbm,
    residual_hbm,
    queries_hbm,
    cache_hbm,
    gate_hbm,
    up_hbm,
    down_hbm,
    mixed_ref,
    attended_hbm,
    weights,
    hidden,
    residual,
    queries,
    cache,
    attended,
    visible,
    order_in,
    order_out,
    mix_high,
    mix_low,
    staged,
    arrived,
    rows,
    projected,
    activated,
    own_part,
    part_send,
    part_recv,
    back_send,
    back_recv,
    load_sem,
    weight_sem,
    out_sem,
    give_send,
    give_recv,
    pass_send,
    pass_recv,
    part_ssem,
    part_rsem,
    back_ssem,
    back_rsem,
):
    sec = lax.axis_index("sec")
    chip = sec // 2
    core = sec % 2
    partner = {"sec": chip * 2 + (1 - core)}
    tokens, width = hidden.shape
    blocks = width // BLOCK
    halves = activated.shape[1] // BLOCK
    sources = 2 * chips
    items = sources * CAP
    own_rows = chips * CAP
    mine = chips * CAP * SUB

    def chip_after(d):
        return (chip + d) % chips

    def chip_before(d):
        return (chip + chips - d) % chips

    def peer(d):
        return {"sec": chip_after(d) * 2 + core}

    barrier = pltpu.get_barrier_semaphore()
    for d in range(1, chips):
        pl.semaphore_signal(barrier, inc=1, device_id=peer(d), device_id_type=MESH)
    pl.semaphore_signal(barrier, inc=1, device_id=partner, device_id_type=MESH)

    loads = [
        pltpu.make_async_copy(src, dst, load_sem.at[i])
        for i, (src, dst) in enumerate(
            ((hidden_hbm, hidden), (queries_hbm, queries), (cache_hbm, cache), (residual_hbm, residual))
        )
    ]
    for load in loads:
        load.start()

    per = 2 * halves

    def first_tile(j, q, slot):
        source = gate_hbm if q % 2 == 0 else up_hbm
        return pltpu.make_async_copy(
            source.at[pl.ds(pl.multiple_of(j * BLOCK, BLOCK), BLOCK), pl.ds((q // 2) * BLOCK, BLOCK)],
            weights.at[slot],
            weight_sem.at[slot],
        )

    def second_tile(j, h, slot):
        return pltpu.make_async_copy(
            down_hbm.at[pl.ds(h * BLOCK, BLOCK), pl.ds(pl.multiple_of(j * BLOCK, BLOCK), BLOCK)],
            weights.at[slot],
            weight_sem.at[slot],
        )

    def fill(j, carry):
        for q in range(per):
            first_tile(j, q, per * j + q).start()
        return carry

    lax.fori_loop(0, SLOTS // per, fill, 0)

    ids = ids_ref[...]
    raised = jax.nn.sigmoid(logits_ref[...])
    gate_weight = raised / jnp.sum(raised, axis=1, keepdims=True)
    column = iota((tokens, mine), 1)
    expert = column // (CAP * SUB)
    position = (column // SUB) % CAP
    named = jnp.zeros((tokens, mine), jnp.float32)
    weight = jnp.zeros((tokens, mine), jnp.float32)
    for choice in range(TOP):
        hit = ids[:, choice : choice + 1] == expert
        named = named + jnp.where(hit, 1.0, 0.0)
        weight = weight + jnp.where(hit, gate_weight[:, choice : choice + 1], 0.0)
    row = iota((tokens, mine), 0)
    earlier = jnp.zeros((tokens, mine), jnp.float32)
    for t in range(tokens - 1):
        earlier = earlier + jnp.where(row > t, named[t : t + 1, :], 0.0)
    taken = jnp.where(earlier == position.astype(jnp.float32), named, 0.0)
    weight = weight * taken
    if tokens < 8:
        blank = jnp.zeros((8 - tokens, mine), jnp.float32)
        taken = jnp.concatenate([taken, blank], axis=0)
        weight = jnp.concatenate([weight, blank], axis=0)
    piece = iota((8, mine), 1) % SUB
    select = jnp.concatenate([jnp.where(piece == i, taken, 0.0) for i in range(SUB)], axis=0)
    mix = jnp.concatenate([jnp.where(piece == i, weight, 0.0) for i in range(SUB)], axis=0)
    high = mix.astype(jnp.bfloat16)
    mix_high[...] = high
    mix_low[...] = (mix - high.astype(jnp.float32)).astype(jnp.bfloat16)

    loads[0].wait()
    full = hidden[...].astype(jnp.float32)
    if tokens < 8:
        full = jnp.concatenate([full, jnp.zeros((8 - tokens, width), jnp.float32)], axis=0)
    stacked = jnp.concatenate(
        [
            jnp.concatenate(
                [full[:, j * BLOCK + i * LANES : j * BLOCK + (i + 1) * LANES] for j in range(blocks)], axis=1
            )
            for i in range(SUB)
        ],
        axis=0,
    ).astype(jnp.bfloat16)
    packed = lax.dot_general(
        select.astype(jnp.bfloat16), stacked, (((0,), (0,)), ((), ())), preferred_element_type=jnp.float32
    )
    staged[...] = packed.astype(jnp.bfloat16).reshape(staged.shape)

    pl.semaphore_wait(barrier, chips)

    def give(d):
        return pltpu.make_async_remote_copy(
            src_ref=staged.at[chip_after(d)],
            dst_ref=arrived.at[core, chip],
            send_sem=give_send.at[d],
            recv_sem=give_recv.at[d],
            device_id=peer(d),
            device_id_type=MESH,
        )

    def hand_over(d):
        source = staged.at[chip] if d == 0 else arrived.at[core, chip_before(d)]
        return pltpu.make_async_remote_copy(
            src_ref=source,
            dst_ref=arrived.at[core, chip_before(d)],
            send_sem=pass_send.at[d],
            recv_sem=pass_recv.at[d],
            device_id=partner,
            device_id_type=MESH,
        )

    for d in range(1, chips):
        give(d).start()
    hand_over(0).start()
    arrived[core, chip] = staged[chip]

    count = items * SUB
    to, frm = iota((count, count), 0), iota((count, count), 1)
    wanted = ((to % items) // CAP) * (CAP * SUB) + (to % CAP) * SUB + to // items
    order_in[...] = jnp.where(frm == wanted, 1.0, 0.0).astype(jnp.bfloat16)
    to, frm = iota((mine, mine), 0), iota((mine, mine), 1)
    wanted = (to % SUB) * own_rows + to // SUB
    order_out[...] = jnp.where(frm == wanted, 1.0, 0.0).astype(jnp.bfloat16)

    requests, held, both = cache.shape
    head = both // 2
    heads = queries.shape[1] // head
    span = requests * held
    request = iota((requests, span), 0)
    place = iota((requests, span), 1)
    slot_of = jnp.zeros((requests, span), jnp.int32)
    length_of = jnp.zeros((requests, span), jnp.int32)
    for r in range(requests):
        slot_of = jnp.where(request == r, slot_ref[0, r], slot_of)
        length_of = jnp.where(request == r, length_ref[r], length_of)
    seen = (place // held == slot_of) & (place % held < length_of)
    visible[...] = jnp.where(seen, 1.0, 0.0)
    loads[1].wait()
    loads[2].wait()
    inverse_root = 1.0 / math.sqrt(head)

    def attend(g, carry):
        base = pl.multiple_of(g * (HEADS_STEP * head), HEADS_STEP * head)
        asked = jnp.concatenate(
            [queries[:, pl.ds(base + h * head, head)].astype(jnp.float32) for h in range(HEADS_STEP)], axis=0
        )
        keys = cache[:, :, 0:head].reshape(span, head)
        values = cache[:, :, head:both].reshape(span, head)
        new_key = jnp.concatenate([new_ref[:, 0:head].astype(jnp.float32)] * HEADS_STEP, axis=0)
        new_value = jnp.concatenate([new_ref[:, head:both].astype(jnp.float32)] * HEADS_STEP, axis=0)
        shown = jnp.concatenate([visible[...]] * HEADS_STEP, axis=0) > 0.5
        scores = (
            lax.dot_general(
                asked.astype(jnp.bfloat16), keys, (((1,), (1,)), ((), ())), preferred_element_type=jnp.float32
            )
            * inverse_root
        )
        scores = jnp.where(shown, scores, NEG_FILL)
        own = jnp.sum(asked * new_key, axis=1, keepdims=True) * inverse_root
        top = jnp.maximum(jnp.max(scores, axis=1, keepdims=True), own)
        lifted = jnp.where(shown, jnp.exp(scores - top), 0.0)
        own_lift = jnp.exp(own - top)
        scale = 1.0 / (jnp.sum(lifted, axis=1, keepdims=True) + own_lift)
        chances = (lifted * scale).astype(jnp.bfloat16)
        own_chance = (own_lift * scale).astype(jnp.bfloat16).astype(jnp.float32)
        result = jnp.dot(chances, values, preferred_element_type=jnp.float32) + own_chance * new_value
        for h in range(HEADS_STEP):
            attended[:, pl.ds(base + h * head, head)] = result[h * requests : (h + 1) * requests].astype(
                jnp.bfloat16
            )
        return carry

    steps = heads // HEADS_STEP
    lax.fori_loop(0, steps // 2, attend, 0)
    for d in range(1, chips):
        give(d).wait_recv()
        hand_over(d).start()
    lax.fori_loop(steps // 2, steps, attend, 0)
    finished = pltpu.make_async_copy(attended, attended_hbm, out_sem)
    finished.start()
    for d in range(chips):
        hand_over(d).wait_recv()

    ordered = jnp.dot(
        order_in[...], arrived[...].reshape(count, blocks * LANES), preferred_element_type=jnp.float32
    ).astype(jnp.bfloat16)
    for j in range(blocks):
        for i in range(SUB):
            rows[j, :, i * LANES : (i + 1) * LANES] = ordered[
                i * items : (i + 1) * items, j * LANES : (j + 1) * LANES
            ]

    projected[...] = jnp.zeros_like(projected)

    def first(j, carry):
        taken_rows = rows[j]
        for q in range(per):
            slot = (per * j + q) % SLOTS
            first_tile(j, q, slot).wait()
            projected[q] += jnp.dot(taken_rows, weights[slot], preferred_element_type=jnp.float32)
            later = j + SLOTS // per

            @pl.when(later < blocks)
            def _():
                first_tile(later, q, slot).start()

            tile = per * (later - blocks) + q

            @pl.when((later >= blocks) & (tile < blocks * halves))
            def _():
                second_tile(tile // halves, q % halves, slot).start()

        return carry

    lax.fori_loop(0, blocks, first, 0)
    for h in range(halves):
        gate_proj, up_proj = projected[2 * h], projected[2 * h + 1]
        activated[:, h * BLOCK : (h + 1) * BLOCK] = (
            gate_proj / (1.0 + jnp.exp(-gate_proj)) * up_proj
        ).astype(jnp.bfloat16)

    def exchange(j):
        return pltpu.make_async_remote_copy(
            src_ref=part_send.at[j],
            dst_ref=part_recv.at[j],
            send_sem=part_ssem.at[j],
            recv_sem=part_rsem.at[j],
            device_id=partner,
            device_id_type=MESH,
        )

    def give_back(j, d):
        return pltpu.make_async_remote_copy(
            src_ref=back_send.at[j, chip_after(d)],
            dst_ref=back_recv.at[j, chip],
            send_sem=back_ssem.at[j, d],
            recv_sem=back_rsem.at[j, d],
            device_id=peer(d),
            device_id_type=MESH,
        )

    def second(j):
        total = jnp.zeros((items, BLOCK), jnp.float32)
        for h in range(halves):
            slot = (blocks * per + halves * j + h) % SLOTS
            second_tile(j, h, slot).wait()
            total = total + jnp.dot(
                activated[:, h * BLOCK : (h + 1) * BLOCK], weights[slot], preferred_element_type=jnp.float32
            )
        here, there = total[0:own_rows], total[own_rows:items]
        part_send[j] = jnp.where(core == 0, there, here).astype(jnp.bfloat16)
        own_part[j] = jnp.where(core == 0, here, there)
        exchange(j).start()

    def send_back(j):
        exchange(j).wait_recv()
        summed = (own_part[j] + part_recv[j].astype(jnp.float32)).astype(jnp.bfloat16)
        pieces = jnp.concatenate([summed[:, i * LANES : (i + 1) * LANES] for i in range(SUB)], axis=0)
        back_send[j] = (
            jnp.dot(order_out[...], pieces, preferred_element_type=jnp.float32)
            .astype(jnp.bfloat16)
            .reshape(chips, CAP * SUB, LANES)
        )
        for d in range(1, chips):
            give_back(j, d).start()
        back_recv[j, chip] = back_send[j, chip]

    def combine(j):
        for d in range(1, chips):
            give_back(j, d).wait_recv()
        returned = back_recv[j].reshape(mine, LANES)
        total = jnp.dot(mix_high[...], returned, preferred_element_type=jnp.float32) + jnp.dot(
            mix_low[...], returned, preferred_element_type=jnp.float32
        )
        base = pl.multiple_of(j * BLOCK, BLOCK)
        for i in range(SUB):
            at = pl.ds(base + i * LANES, LANES)
            mixed_ref[:, at] = (
                residual[:, at].astype(jnp.float32) + total[i * 8 : i * 8 + tokens]
            ).astype(jnp.bfloat16)

    loads[3].wait()

    def down(j, carry):
        second(j)

        @pl.when(j >= 1)
        def _():
            send_back(j - 1)

        @pl.when(j >= 2)
        def _():
            combine(j - 2)

        return carry

    lax.fori_loop(0, blocks, down, 0)
    send_back(blocks - 1)
    combine(blocks - 2)
    combine(blocks - 1)

    for d in range(1, chips):
        give(d).wait_send()
    for d in range(chips):
        hand_over(d).wait_send()

    def drain(j, carry):
        exchange(j).wait_send()
        for d in range(1, chips):
            give_back(j, d).wait_send()
        return carry

    lax.fori_loop(0, blocks, drain, 0)
    finished.wait()


def fused_layer(
    hidden_rows,
    residual,
    expert_ids,
    router_logits,
    w_gate,
    w_up,
    w_down,
    queries,
    new_kv,
    kv_cache,
    cache_slot,
    cache_lengths,
):
    chips = lax.axis_size("sec") // 2
    tokens, width = hidden_rows.shape
    hidden_each = w_gate.shape[1]
    blocks = width // BLOCK
    halves = hidden_each // BLOCK
    requests, held, both = kv_cache.shape
    items = 2 * chips * CAP
    mine = chips * CAP * SUB
    vmem = pl.BlockSpec(memory_space=pltpu.VMEM)
    smem = pl.BlockSpec(memory_space=pltpu.SMEM)
    anywhere = pl.BlockSpec(memory_space=pl.ANY)
    bf16, f32 = jnp.bfloat16, jnp.float32
    dma = pltpu.SemaphoreType.DMA
    return pl.pallas_call(
        functools.partial(layer_kernel, chips),
        out_shape=(
            jax.ShapeDtypeStruct((tokens, width), bf16),
            jax.ShapeDtypeStruct(queries.shape, bf16),
        ),
        in_specs=[vmem, vmem, vmem, smem, smem] + [anywhere] * 7,
        out_specs=(vmem, anywhere),
        scratch_shapes=[
            pltpu.VMEM((SLOTS, BLOCK, BLOCK), bf16),
            pltpu.VMEM((tokens, width), bf16),
            pltpu.VMEM((tokens, width), bf16),
            pltpu.VMEM(queries.shape, bf16),
            pltpu.VMEM(kv_cache.shape, bf16),
            pltpu.VMEM(queries.shape, bf16),
            pltpu.VMEM((requests, requests * held), f32),
            pltpu.VMEM((items * SUB, items * SUB), bf16),
            pltpu.VMEM((mine, mine), bf16),
            pltpu.VMEM((8 * SUB, mine), bf16),
            pltpu.VMEM((8 * SUB, mine), bf16),
            pltpu.VMEM((chips, CAP * SUB, blocks * LANES), bf16),
            pltpu.VMEM((2, chips, CAP * SUB, blocks * LANES), bf16),
            pltpu.VMEM((blocks, items, BLOCK), bf16),
            pltpu.VMEM((2 * halves, items, BLOCK), f32),
            pltpu.VMEM((items, hidden_each), bf16),
            pltpu.VMEM((blocks, chips * CAP, BLOCK), f32),
            pltpu.VMEM((blocks, chips * CAP, BLOCK), bf16),
            pltpu.VMEM((blocks, chips * CAP, BLOCK), bf16),
            pltpu.VMEM((blocks, chips, CAP * SUB, LANES), bf16),
            pltpu.VMEM((blocks, chips, CAP * SUB, LANES), bf16),
            dma((4,)),
            dma((SLOTS,)),
            dma,
            dma((chips,)),
            dma((chips,)),
            dma((chips,)),
            dma((chips,)),
            dma((blocks,)),
            dma((blocks,)),
            dma((blocks, chips)),
            dma((blocks, chips)),
        ],
        compiler_params=pltpu.CompilerParams(
            collective_id=0, has_side_effects=True, vmem_limit_bytes=VMEM_BYTES
        ),
        cost_estimate=pl.CostEstimate(
            flops=6 * items * width * hidden_each,
            bytes_accessed=6 * width * hidden_each,
            transcendentals=0,
        ),
    )(
        expert_ids,
        router_logits,
        new_kv,
        cache_slot,
        cache_lengths,
        hidden_rows,
        residual,
        queries,
        kv_cache,
        w_gate,
        w_up,
        w_down,
    )


def slot_codes(expert_ids, capacity):
    flattened = expert_ids.reshape(-1)
    onehot = (flattened[:, None] == jnp.arange(EXPERTS, dtype=jnp.int32)[None, :]).astype(jnp.int32)
    earlier = jnp.cumsum(onehot, axis=0) - onehot
    position = jnp.sum(earlier * onehot, axis=1)
    return (flattened * capacity + position).reshape(expert_ids.shape)


def plain_layer(
    hidden_rows,
    residual,
    expert_ids,
    router_logits,
    w_gate,
    w_up,
    w_down,
    queries,
    new_kv,
    kv_cache,
    cache_slot,
    cache_lengths,
):
    devices = lax.axis_size("sec")
    shards = devices // EXPERTS
    tokens_here = hidden_rows.shape[0]
    model_width = hidden_rows.shape[1]
    capacity = CAP
    columns = EXPERTS * capacity
    coded = slot_codes(expert_ids, capacity)
    raised = jax.nn.sigmoid(router_logits)
    gate_weight = raised / jnp.sum(raised, axis=1, keepdims=True)
    picked = coded[:, :, None] == jnp.arange(columns, dtype=jnp.int32)[None, None, :]
    select = jnp.sum(picked, axis=1).astype(jnp.bfloat16)
    packed = jnp.einsum(
        "tc,td->cd", select, hidden_rows, preferred_element_type=jnp.float32
    ).astype(jnp.bfloat16)
    outgoing = jnp.broadcast_to(
        packed.reshape(EXPERTS, 1, capacity, model_width), (EXPERTS, shards, capacity, model_width)
    )
    outgoing = outgoing.reshape(devices, capacity, model_width)
    arrived = lax.all_to_all(outgoing, "sec", split_axis=0, concat_axis=0, tiled=True)
    items = arrived.shape[1]
    flattened = arrived.reshape(-1, model_width)
    gate_proj = jnp.dot(flattened, w_gate, preferred_element_type=jnp.float32)
    up_proj = jnp.dot(flattened, w_up, preferred_element_type=jnp.float32)
    activated = (jax.nn.silu(gate_proj) * up_proj).astype(jnp.bfloat16)
    partial_value = jnp.dot(activated, w_down, preferred_element_type=jnp.float32).astype(
        jnp.bfloat16
    )
    partial_value = partial_value.reshape(devices, items, model_width)
    returned = lax.all_to_all(partial_value, "sec", split_axis=0, concat_axis=0, tiled=True)
    gathered = jnp.sum(
        returned.astype(jnp.float32).reshape(EXPERTS, shards, capacity, model_width), axis=1
    ).reshape(columns, model_width)
    chosen_rows = gathered[coded.reshape(-1)].reshape(tokens_here, TOP, model_width)
    mixed = (
        residual.astype(jnp.float32) + jnp.sum(gate_weight[:, :, None] * chosen_rows, axis=1)
    ).astype(jnp.bfloat16)
    requests_here = queries.shape[0]
    head_size = new_kv.shape[1] // 2
    head_count = queries.shape[1] // head_size
    positions = kv_cache.shape[1]
    cache_rows = kv_cache[cache_slot.reshape(-1)]
    cache_keys = cache_rows[:, :, :head_size]
    cache_values = cache_rows[:, :, head_size:]
    query_heads = queries.reshape(requests_here, head_count, head_size)
    inverse_root = 1.0 / math.sqrt(head_size)
    scores = (
        jnp.einsum("rhd,rcd->rhc", query_heads, cache_keys, preferred_element_type=jnp.float32)
        * inverse_root
    )
    own_score = (
        jnp.einsum(
            "rhd,rd->rh", query_heads, new_kv[:, :head_size], preferred_element_type=jnp.float32
        )
        * inverse_root
    )
    visible = jnp.arange(positions, dtype=jnp.int32)[None, None, :] < cache_lengths[:, None, None]
    scores = jnp.where(visible, scores, NEG_FILL)
    row_max = jnp.maximum(jnp.max(scores, axis=2), own_score)
    lifted = jnp.where(visible, jnp.exp(scores - row_max[:, :, None]), 0.0)
    own_lift = jnp.exp(own_score - row_max)
    denominator = jnp.sum(lifted, axis=2) + own_lift
    weights_bf = (lifted / denominator[:, :, None]).astype(jnp.bfloat16)
    own_bf = (own_lift / denominator).astype(jnp.bfloat16)
    combined = jnp.einsum(
        "rhc,rcd->rhd", weights_bf, cache_values, preferred_element_type=jnp.float32
    )
    combined = (
        combined
        + own_bf.astype(jnp.float32)[:, :, None]
        * new_kv[:, head_size:].astype(jnp.float32)[:, None, :]
    )
    attended = combined.astype(jnp.bfloat16).reshape(requests_here, head_count * head_size)
    return (mixed, attended)


def per_device(hidden_rows, residual, expert_ids, router_logits, w_gate, w_up, w_down, queries, *rest):
    fits = (
        lax.axis_size("sec") == 2 * EXPERTS
        and hidden_rows.shape[0] <= 8
        and hidden_rows.shape[1] % BLOCK == 0
        and w_gate.shape[1] == 2 * BLOCK
        and SLOTS // 4 <= hidden_rows.shape[1] // BLOCK
    )
    layer = fused_layer if fits else plain_layer
    return layer(hidden_rows, residual, expert_ids, router_logits, w_gate, w_up, w_down, queries, *rest)


def solution(mesh):
    placed = (
        P(("groups", "sec"), None),
        P(("groups", "sec"), None),
        P(("groups", "sec"), None),
        P(("groups", "sec"), None),
        P(None, "sec"),
        P(None, "sec"),
        P("sec", None),
        P(("groups", "sec"), None),
        P(("groups", "sec"), None),
        P(("groups", "sec"), None, None),
        P(("groups", "sec"), None),
        P(("groups", "sec")),
    )
    return jax.shard_map(
        per_device,
        mesh=mesh,
        in_specs=placed,
        out_specs=(P(("groups", "sec"), None), P(("groups", "sec"), None)),
        check_vma=False,
    )
```

```python
import functools
import math

import jax
import jax.numpy as jnp
from jax import lax
from jax.experimental import pallas as pl
from jax.experimental.pallas import tpu as pltpu
from jax.sharding import PartitionSpec as P

EXPERTS = 8
TOP = 3
CAP = 2

NEG_FILL = -1e30

LANES = 128
SUB = 8
BLOCK = SUB * LANES
VMEM_BYTES = 63 * 1024 * 1024
SLOTS = 28
HEADS_STEP = 16
GROUPS = ((0, 3), (3, 5), (5, 7))
MESH = pl.DeviceIdType.MESH


def iota(shape, dim):
    return lax.broadcasted_iota(jnp.int32, shape, dim)


def layer_kernel(
    chips,
    ids_ref,
    logits_ref,
    new_ref,
    slot_ref,
    length_ref,
    hidden_hbm,
    residual_hbm,
    queries_hbm,
    cache_hbm,
    gate_hbm,
    up_hbm,
    down_hbm,
    mixed_ref,
    attended_hbm,
    weights,
    hidden,
    residual,
    queries,
    cache,
    attended,
    visible,
    order_in,
    order_out,
    mix_high,
    mix_low,
    staged,
    arrived,
    rows,
    projected,
    activated,
    own_part,
    part_send,
    part_recv,
    back_send,
    back_recv,
    load_sem,
    weight_sem,
    out_sem,
    give_send,
    give_recv,
    pass_send,
    pass_recv,
    part_ssem,
    part_rsem,
    back_ssem,
    back_rsem,
):
    sec = lax.axis_index("sec")
    chip = sec // 2
    core = sec % 2
    partner = {"sec": chip * 2 + (1 - core)}
    tokens, width = hidden.shape
    blocks = width // BLOCK
    halves = activated.shape[1] // BLOCK
    sources = 2 * chips
    items = sources * CAP
    own_rows = chips * CAP
    mine = chips * CAP * SUB

    def chip_after(d):
        return (chip + d) % chips

    def chip_before(d):
        return (chip + chips - d) % chips

    def peer(d):
        return {"sec": chip_after(d) * 2 + core}

    barrier = pltpu.get_barrier_semaphore()
    for d in range(1, chips):
        pl.semaphore_signal(barrier, inc=1, device_id=peer(d), device_id_type=MESH)
    pl.semaphore_signal(barrier, inc=1, device_id=partner, device_id_type=MESH)

    loads = [
        pltpu.make_async_copy(src, dst, load_sem.at[i])
        for i, (src, dst) in enumerate(
            ((hidden_hbm, hidden), (queries_hbm, queries), (cache_hbm, cache), (residual_hbm, residual))
        )
    ]
    for load in loads:
        load.start()

    per = 2 * halves

    def first_tile(j, q, slot):
        source = gate_hbm if q % 2 == 0 else up_hbm
        return pltpu.make_async_copy(
            source.at[pl.ds(pl.multiple_of(j * BLOCK, BLOCK), BLOCK), pl.ds((q // 2) * BLOCK, BLOCK)],
            weights.at[slot],
            weight_sem.at[slot],
        )

    def second_tile(j, h, slot):
        return pltpu.make_async_copy(
            down_hbm.at[pl.ds(h * BLOCK, BLOCK), pl.ds(pl.multiple_of(j * BLOCK, BLOCK), BLOCK)],
            weights.at[slot],
            weight_sem.at[slot],
        )

    def fill(j, carry):
        for q in range(per):
            first_tile(j, q, per * j + q).start()
        return carry

    lax.fori_loop(0, SLOTS // per, fill, 0)

    ids = ids_ref[...]
    raised = jax.nn.sigmoid(logits_ref[...])
    gate_weight = raised / jnp.sum(raised, axis=1, keepdims=True)
    column = iota((tokens, mine), 1)
    expert = column // (CAP * SUB)
    position = (column // SUB) % CAP
    named = jnp.zeros((tokens, mine), jnp.float32)
    weight = jnp.zeros((tokens, mine), jnp.float32)
    for choice in range(TOP):
        hit = ids[:, choice : choice + 1] == expert
        named = named + jnp.where(hit, 1.0, 0.0)
        weight = weight + jnp.where(hit, gate_weight[:, choice : choice + 1], 0.0)
    row = iota((tokens, mine), 0)
    earlier = jnp.zeros((tokens, mine), jnp.float32)
    for t in range(tokens - 1):
        earlier = earlier + jnp.where(row > t, named[t : t + 1, :], 0.0)
    taken = jnp.where(earlier == position.astype(jnp.float32), named, 0.0)
    weight = weight * taken
    if tokens < 8:
        blank = jnp.zeros((8 - tokens, mine), jnp.float32)
        taken = jnp.concatenate([taken, blank], axis=0)
        weight = jnp.concatenate([weight, blank], axis=0)
    piece = iota((8, mine), 1) % SUB
    select = jnp.concatenate([jnp.where(piece == i, taken, 0.0) for i in range(SUB)], axis=0)
    mix = jnp.concatenate([jnp.where(piece == i, weight, 0.0) for i in range(SUB)], axis=0)
    high = mix.astype(jnp.bfloat16)
    mix_high[...] = high
    mix_low[...] = (mix - high.astype(jnp.float32)).astype(jnp.bfloat16)

    loads[0].wait()
    full = hidden[...].astype(jnp.float32)
    if tokens < 8:
        full = jnp.concatenate([full, jnp.zeros((8 - tokens, width), jnp.float32)], axis=0)
    stacked = jnp.concatenate(
        [
            jnp.concatenate(
                [full[:, j * BLOCK + i * LANES : j * BLOCK + (i + 1) * LANES] for j in range(blocks)], axis=1
            )
            for i in range(SUB)
        ],
        axis=0,
    ).astype(jnp.bfloat16)
    packed = lax.dot_general(
        select.astype(jnp.bfloat16), stacked, (((0,), (0,)), ((), ())), preferred_element_type=jnp.float32
    )
    staged[...] = packed.astype(jnp.bfloat16).reshape(staged.shape)

    pl.semaphore_wait(barrier, chips)

    def give(d):
        return pltpu.make_async_remote_copy(
            src_ref=staged.at[chip_after(d)],
            dst_ref=arrived.at[core, chip],
            send_sem=give_send.at[d],
            recv_sem=give_recv.at[d],
            device_id=peer(d),
            device_id_type=MESH,
        )

    def hand_over(d):
        source = staged.at[chip] if d == 0 else arrived.at[core, chip_before(d)]
        return pltpu.make_async_remote_copy(
            src_ref=source,
            dst_ref=arrived.at[core, chip_before(d)],
            send_sem=pass_send.at[d],
            recv_sem=pass_recv.at[d],
            device_id=partner,
            device_id_type=MESH,
        )

    for d in range(1, chips):
        give(d).start()
    hand_over(0).start()
    arrived[core, chip] = staged[chip]

    count = items * SUB
    to, frm = iota((count, count), 0), iota((count, count), 1)
    wanted = ((to % items) // CAP) * (CAP * SUB) + (to % CAP) * SUB + to // items
    order_in[...] = jnp.where(frm == wanted, 1.0, 0.0).astype(jnp.bfloat16)
    to, frm = iota((mine, mine), 0), iota((mine, mine), 1)
    wanted = (to % SUB) * own_rows + to // SUB
    order_out[...] = jnp.where(frm == wanted, 1.0, 0.0).astype(jnp.bfloat16)

    requests, held, both = cache.shape
    head = both // 2
    heads = queries.shape[1] // head
    span = requests * held
    request = iota((requests, span), 0)
    place = iota((requests, span), 1)
    slot_of = jnp.zeros((requests, span), jnp.int32)
    length_of = jnp.zeros((requests, span), jnp.int32)
    for r in range(requests):
        slot_of = jnp.where(request == r, slot_ref[0, r], slot_of)
        length_of = jnp.where(request == r, length_ref[r], length_of)
    seen = (place // held == slot_of) & (place % held < length_of)
    visible[...] = jnp.where(seen, 1.0, 0.0)
    loads[1].wait()
    loads[2].wait()
    inverse_root = 1.0 / math.sqrt(head)

    def attend(g, carry):
        base = pl.multiple_of(g * (HEADS_STEP * head), HEADS_STEP * head)
        asked = jnp.concatenate(
            [queries[:, pl.ds(base + h * head, head)].astype(jnp.float32) for h in range(HEADS_STEP)], axis=0
        )
        keys = cache[:, :, 0:head].reshape(span, head)
        values = cache[:, :, head:both].reshape(span, head)
        new_key = jnp.concatenate([new_ref[:, 0:head].astype(jnp.float32)] * HEADS_STEP, axis=0)
        new_value = jnp.concatenate([new_ref[:, head:both].astype(jnp.float32)] * HEADS_STEP, axis=0)
        shown = jnp.concatenate([visible[...]] * HEADS_STEP, axis=0) > 0.5
        scores = (
            lax.dot_general(
                asked.astype(jnp.bfloat16), keys, (((1,), (1,)), ((), ())), preferred_element_type=jnp.float32
            )
            * inverse_root
        )
        scores = jnp.where(shown, scores, NEG_FILL)
        own = jnp.sum(asked * new_key, axis=1, keepdims=True) * inverse_root
        top = jnp.maximum(jnp.max(scores, axis=1, keepdims=True), own)
        lifted = jnp.where(shown, jnp.exp(scores - top), 0.0)
        own_lift = jnp.exp(own - top)
        scale = 1.0 / (jnp.sum(lifted, axis=1, keepdims=True) + own_lift)
        chances = (lifted * scale).astype(jnp.bfloat16)
        own_chance = (own_lift * scale).astype(jnp.bfloat16).astype(jnp.float32)
        result = jnp.dot(chances, values, preferred_element_type=jnp.float32) + own_chance * new_value
        for h in range(HEADS_STEP):
            attended[:, pl.ds(base + h * head, head)] = result[h * requests : (h + 1) * requests].astype(
                jnp.bfloat16
            )
        return carry

    steps = heads // HEADS_STEP
    lax.fori_loop(0, steps // 2, attend, 0)
    for d in range(1, chips):
        give(d).wait_recv()
        hand_over(d).start()
    lax.fori_loop(steps // 2, steps, attend, 0)
    finished = pltpu.make_async_copy(attended, attended_hbm, out_sem)
    finished.start()
    for d in range(chips):
        hand_over(d).wait_recv()

    ordered = jnp.dot(
        order_in[...], arrived[...].reshape(count, blocks * LANES), preferred_element_type=jnp.float32
    ).astype(jnp.bfloat16)
    for j in range(blocks):
        for i in range(SUB):
            rows[j, :, i * LANES : (i + 1) * LANES] = ordered[
                i * items : (i + 1) * items, j * LANES : (j + 1) * LANES
            ]

    projected[...] = jnp.zeros_like(projected)

    def first(j, carry):
        taken_rows = rows[j]
        for q in range(per):
            slot = (per * j + q) % SLOTS
            first_tile(j, q, slot).wait()
            projected[q] += jnp.dot(taken_rows, weights[slot], preferred_element_type=jnp.float32)
            later = j + SLOTS // per

            @pl.when(later < blocks)
            def _():
                first_tile(later, q, slot).start()

            tile = per * (later - blocks) + q

            @pl.when((later >= blocks) & (tile < blocks * halves))
            def _():
                second_tile(tile // halves, q % halves, slot).start()

        return carry

    lax.fori_loop(0, blocks, first, 0)
    for h in range(halves):
        gate_proj, up_proj = projected[2 * h], projected[2 * h + 1]
        activated[:, h * BLOCK : (h + 1) * BLOCK] = (
            gate_proj / (1.0 + jnp.exp(-gate_proj)) * up_proj
        ).astype(jnp.bfloat16)

    def exchange(j):
        return pltpu.make_async_remote_copy(
            src_ref=part_send.at[j],
            dst_ref=part_recv.at[j],
            send_sem=part_ssem.at[j],
            recv_sem=part_rsem.at[j],
            device_id=partner,
            device_id_type=MESH,
        )

    def lanes(j):
        return pl.ds(pl.multiple_of(j * LANES, LANES), LANES)

    def give_back(g, d):
        low, high = GROUPS[g]
        span = pl.ds(low * LANES, (high - low) * LANES)
        return pltpu.make_async_remote_copy(
            src_ref=back_send.at[chip_after(d), :, span],
            dst_ref=back_recv.at[chip, :, span],
            send_sem=back_ssem.at[g, d],
            recv_sem=back_rsem.at[g, d],
            device_id=peer(d),
            device_id_type=MESH,
        )

    def second(j):
        total = jnp.zeros((items, BLOCK), jnp.float32)
        for h in range(halves):
            slot = (blocks * per + halves * j + h) % SLOTS
            second_tile(j, h, slot).wait()
            total = total + jnp.dot(
                activated[:, h * BLOCK : (h + 1) * BLOCK], weights[slot], preferred_element_type=jnp.float32
            )
        here, there = total[0:own_rows], total[own_rows:items]
        part_send[j] = jnp.where(core == 0, there, here).astype(jnp.bfloat16)
        own_part[j] = jnp.where(core == 0, here, there)
        exchange(j).start()

    def send_back(j):
        exchange(j).wait_recv()
        summed = (own_part[j] + part_recv[j].astype(jnp.float32)).astype(jnp.bfloat16)
        pieces = jnp.concatenate([summed[:, i * LANES : (i + 1) * LANES] for i in range(SUB)], axis=0)
        back_send[:, :, lanes(j)] = (
            jnp.dot(order_out[...], pieces, preferred_element_type=jnp.float32)
            .astype(jnp.bfloat16)
            .reshape(chips, CAP * SUB, LANES)
        )
        back_recv[chip, :, lanes(j)] = back_send[chip, :, lanes(j)]
        for g, (low, high) in enumerate(GROUPS):

            @pl.when(j == high - 1)
            def _():
                for d in range(1, chips):
                    give_back(g, d).start()

    def combine(j):
        returned = back_recv[:, :, lanes(j)].reshape(mine, LANES)
        total = jnp.dot(mix_high[...], returned, preferred_element_type=jnp.float32) + jnp.dot(
            mix_low[...], returned, preferred_element_type=jnp.float32
        )
        base = pl.multiple_of(j * BLOCK, BLOCK)
        for i in range(SUB):
            at = pl.ds(base + i * LANES, LANES)
            mixed_ref[:, at] = (
                residual[:, at].astype(jnp.float32) + total[i * 8 : i * 8 + tokens]
            ).astype(jnp.bfloat16)

    loads[3].wait()

    def down(j, carry):
        second(j)

        @pl.when(j >= 1)
        def _():
            send_back(j - 1)

        return carry

    lax.fori_loop(0, blocks, down, 0)
    send_back(jnp.int32(blocks - 1))
    for g, (low, high) in enumerate(GROUPS):
        for d in range(1, chips):
            give_back(g, d).wait_recv()
        for j in range(low, high):
            combine(jnp.int32(j))

    for d in range(1, chips):
        give(d).wait_send()
    for d in range(chips):
        hand_over(d).wait_send()

    def drain(j, carry):
        exchange(j).wait_send()
        return carry

    lax.fori_loop(0, blocks, drain, 0)
    for g in range(len(GROUPS)):
        for d in range(1, chips):
            give_back(g, d).wait_send()
    finished.wait()


def fused_layer(
    hidden_rows,
    residual,
    expert_ids,
    router_logits,
    w_gate,
    w_up,
    w_down,
    queries,
    new_kv,
    kv_cache,
    cache_slot,
    cache_lengths,
):
    chips = lax.axis_size("sec") // 2
    tokens, width = hidden_rows.shape
    hidden_each = w_gate.shape[1]
    blocks = width // BLOCK
    halves = hidden_each // BLOCK
    requests, held, both = kv_cache.shape
    items = 2 * chips * CAP
    mine = chips * CAP * SUB
    vmem = pl.BlockSpec(memory_space=pltpu.VMEM)
    smem = pl.BlockSpec(memory_space=pltpu.SMEM)
    anywhere = pl.BlockSpec(memory_space=pl.ANY)
    bf16, f32 = jnp.bfloat16, jnp.float32
    dma = pltpu.SemaphoreType.DMA
    return pl.pallas_call(
        functools.partial(layer_kernel, chips),
        out_shape=(
            jax.ShapeDtypeStruct((tokens, width), bf16),
            jax.ShapeDtypeStruct(queries.shape, bf16),
        ),
        in_specs=[vmem, vmem, vmem, smem, smem] + [anywhere] * 7,
        out_specs=(vmem, anywhere),
        scratch_shapes=[
            pltpu.VMEM((SLOTS, BLOCK, BLOCK), bf16),
            pltpu.VMEM((tokens, width), bf16),
            pltpu.VMEM((tokens, width), bf16),
            pltpu.VMEM(queries.shape, bf16),
            pltpu.VMEM(kv_cache.shape, bf16),
            pltpu.VMEM(queries.shape, bf16),
            pltpu.VMEM((requests, requests * held), f32),
            pltpu.VMEM((items * SUB, items * SUB), bf16),
            pltpu.VMEM((mine, mine), bf16),
            pltpu.VMEM((8 * SUB, mine), bf16),
            pltpu.VMEM((8 * SUB, mine), bf16),
            pltpu.VMEM((chips, CAP * SUB, blocks * LANES), bf16),
            pltpu.VMEM((2, chips, CAP * SUB, blocks * LANES), bf16),
            pltpu.VMEM((blocks, items, BLOCK), bf16),
            pltpu.VMEM((2 * halves, items, BLOCK), f32),
            pltpu.VMEM((items, hidden_each), bf16),
            pltpu.VMEM((blocks, chips * CAP, BLOCK), f32),
            pltpu.VMEM((blocks, chips * CAP, BLOCK), bf16),
            pltpu.VMEM((blocks, chips * CAP, BLOCK), bf16),
            pltpu.VMEM((chips, CAP * SUB, blocks * LANES), bf16),
            pltpu.VMEM((chips, CAP * SUB, blocks * LANES), bf16),
            dma((4,)),
            dma((SLOTS,)),
            dma,
            dma((chips,)),
            dma((chips,)),
            dma((chips,)),
            dma((chips,)),
            dma((blocks,)),
            dma((blocks,)),
            dma((len(GROUPS), chips)),
            dma((len(GROUPS), chips)),
        ],
        compiler_params=pltpu.CompilerParams(
            collective_id=0, has_side_effects=True, vmem_limit_bytes=VMEM_BYTES
        ),
        cost_estimate=pl.CostEstimate(
            flops=6 * items * width * hidden_each,
            bytes_accessed=6 * width * hidden_each,
            transcendentals=0,
        ),
    )(
        expert_ids,
        router_logits,
        new_kv,
        cache_slot,
        cache_lengths,
        hidden_rows,
        residual,
        queries,
        kv_cache,
        w_gate,
        w_up,
        w_down,
    )


def slot_codes(expert_ids, capacity):
    flattened = expert_ids.reshape(-1)
    onehot = (flattened[:, None] == jnp.arange(EXPERTS, dtype=jnp.int32)[None, :]).astype(jnp.int32)
    earlier = jnp.cumsum(onehot, axis=0) - onehot
    position = jnp.sum(earlier * onehot, axis=1)
    return (flattened * capacity + position).reshape(expert_ids.shape)


def plain_layer(
    hidden_rows,
    residual,
    expert_ids,
    router_logits,
    w_gate,
    w_up,
    w_down,
    queries,
    new_kv,
    kv_cache,
    cache_slot,
    cache_lengths,
):
    devices = lax.axis_size("sec")
    shards = devices // EXPERTS
    tokens_here = hidden_rows.shape[0]
    model_width = hidden_rows.shape[1]
    capacity = CAP
    columns = EXPERTS * capacity
    coded = slot_codes(expert_ids, capacity)
    raised = jax.nn.sigmoid(router_logits)
    gate_weight = raised / jnp.sum(raised, axis=1, keepdims=True)
    picked = coded[:, :, None] == jnp.arange(columns, dtype=jnp.int32)[None, None, :]
    select = jnp.sum(picked, axis=1).astype(jnp.bfloat16)
    packed = jnp.einsum(
        "tc,td->cd", select, hidden_rows, preferred_element_type=jnp.float32
    ).astype(jnp.bfloat16)
    outgoing = jnp.broadcast_to(
        packed.reshape(EXPERTS, 1, capacity, model_width), (EXPERTS, shards, capacity, model_width)
    )
    outgoing = outgoing.reshape(devices, capacity, model_width)
    arrived = lax.all_to_all(outgoing, "sec", split_axis=0, concat_axis=0, tiled=True)
    items = arrived.shape[1]
    flattened = arrived.reshape(-1, model_width)
    gate_proj = jnp.dot(flattened, w_gate, preferred_element_type=jnp.float32)
    up_proj = jnp.dot(flattened, w_up, preferred_element_type=jnp.float32)
    activated = (jax.nn.silu(gate_proj) * up_proj).astype(jnp.bfloat16)
    partial_value = jnp.dot(activated, w_down, preferred_element_type=jnp.float32).astype(
        jnp.bfloat16
    )
    partial_value = partial_value.reshape(devices, items, model_width)
    returned = lax.all_to_all(partial_value, "sec", split_axis=0, concat_axis=0, tiled=True)
    gathered = jnp.sum(
        returned.astype(jnp.float32).reshape(EXPERTS, shards, capacity, model_width), axis=1
    ).reshape(columns, model_width)
    chosen_rows = gathered[coded.reshape(-1)].reshape(tokens_here, TOP, model_width)
    mixed = (
        residual.astype(jnp.float32) + jnp.sum(gate_weight[:, :, None] * chosen_rows, axis=1)
    ).astype(jnp.bfloat16)
    requests_here = queries.shape[0]
    head_size = new_kv.shape[1] // 2
    head_count = queries.shape[1] // head_size
    positions = kv_cache.shape[1]
    cache_rows = kv_cache[cache_slot.reshape(-1)]
    cache_keys = cache_rows[:, :, :head_size]
    cache_values = cache_rows[:, :, head_size:]
    query_heads = queries.reshape(requests_here, head_count, head_size)
    inverse_root = 1.0 / math.sqrt(head_size)
    scores = (
        jnp.einsum("rhd,rcd->rhc", query_heads, cache_keys, preferred_element_type=jnp.float32)
        * inverse_root
    )
    own_score = (
        jnp.einsum(
            "rhd,rd->rh", query_heads, new_kv[:, :head_size], preferred_element_type=jnp.float32
        )
        * inverse_root
    )
    visible = jnp.arange(positions, dtype=jnp.int32)[None, None, :] < cache_lengths[:, None, None]
    scores = jnp.where(visible, scores, NEG_FILL)
    row_max = jnp.maximum(jnp.max(scores, axis=2), own_score)
    lifted = jnp.where(visible, jnp.exp(scores - row_max[:, :, None]), 0.0)
    own_lift = jnp.exp(own_score - row_max)
    denominator = jnp.sum(lifted, axis=2) + own_lift
    weights_bf = (lifted / denominator[:, :, None]).astype(jnp.bfloat16)
    own_bf = (own_lift / denominator).astype(jnp.bfloat16)
    combined = jnp.einsum(
        "rhc,rcd->rhd", weights_bf, cache_values, preferred_element_type=jnp.float32
    )
    combined = (
        combined
        + own_bf.astype(jnp.float32)[:, :, None]
        * new_kv[:, head_size:].astype(jnp.float32)[:, None, :]
    )
    attended = combined.astype(jnp.bfloat16).reshape(requests_here, head_count * head_size)
    return (mixed, attended)


def per_device(hidden_rows, residual, expert_ids, router_logits, w_gate, w_up, w_down, queries, *rest):
    fits = (
        lax.axis_size("sec") == 2 * EXPERTS
        and hidden_rows.shape[0] <= 8
        and hidden_rows.shape[1] % BLOCK == 0
        and w_gate.shape[1] == 2 * BLOCK
        and hidden_rows.shape[1] // BLOCK == GROUPS[-1][1]
        and SLOTS // 4 <= hidden_rows.shape[1] // BLOCK
    )
    layer = fused_layer if fits else plain_layer
    return layer(hidden_rows, residual, expert_ids, router_logits, w_gate, w_up, w_down, queries, *rest)


def solution(mesh):
    placed = (
        P(("groups", "sec"), None),
        P(("groups", "sec"), None),
        P(("groups", "sec"), None),
        P(("groups", "sec"), None),
        P(None, "sec"),
        P(None, "sec"),
        P("sec", None),
        P(("groups", "sec"), None),
        P(("groups", "sec"), None),
        P(("groups", "sec"), None, None),
        P(("groups", "sec"), None),
        P(("groups", "sec")),
    )
    return jax.shard_map(
        per_device,
        mesh=mesh,
        in_specs=placed,
        out_specs=(P(("groups", "sec"), None), P(("groups", "sec"), None)),
        check_vma=False,
    )
```
